512 devices in a mesh: ctx: 32 (over z_lo, y), tp: 16 (over x, z_hi, core).
Axes of the slice: x: 4, y: 4, z: 16 (z_hi: 2, z_lo: 8; z = z_hi * 8 + z_lo), core: 2. Of those that a mesh axis runs over, the one named last changes fastest.
Arguments:
- queries: bfloat16 [4096, 16384], P('ctx', 'tp'), may hold values from -12 to 12
- new_kv: bfloat16 [4096, 2048], P(('ctx', 'tp')), may hold values from -5 to 5
- cache_kv: bfloat16 [4096, 2048], P(('ctx', 'tp')), may hold values from -5 to 5
- hit_tokens: int32 [32], P('ctx'), may hold values from 1 to 128, 2560 in all
- block_order: int32 [32], P('ctx'), may hold values from 0 to 31, each once
Outputs:
- attended: bfloat16 [4096, 16384], P('ctx', 'tp')
The draws below stay inside these ranges and needn't reach their ends.
Inputs may be any that keep to these rules, and one draw needn't show every extreme that they name: Context group d holds live cache tokens in its first hit_tokens[d] of 128 slots; the counts sum to 2560. `block_order`: each block of the turn is held by exactly one context group.
All inputs are finite; a program needn't handle non-finite values.
Results may differ from the reference program's by a relative error of at most 0.0054.
Values may be sent and summed in bfloat16 or wider, within the bound.
A program may use at most 64 MiB of HBM per device.

```python
import math
import jax
import jax.numpy as jnp
import numpy as np
from jax import lax

HQ = 128
KV = 8
HD = 128
TOK_DEV = 128
CACHE_DEV = 128
NEW = 4096
CACHE = 4096
HITS = 2560
N_CTX = 32


def draw_queries(key, part):
    key = jax.random.fold_in(key, 1)
    return jnp.clip(2.5 * jax.random.normal(key, (NEW, HQ * HD), jnp.float32), -12.0, 12.0).astype(jnp.bfloat16)


def draw_cache_kv(key, part):
    key = jax.random.fold_in(key, 2)
    return jnp.clip(jax.random.normal(key, (CACHE, KV * 2 * HD), jnp.float32), -5.0, 5.0).astype(jnp.bfloat16)


def block_levels(key, extent, cuts, least, high):
    factor_of, own = 1.0, jax.random.fold_in(key, 6)
    for axis_at, shards_of in cuts:
        draws = jnp.exp(jax.random.uniform(jax.random.fold_in(own, axis_at), (shards_of,), jnp.float32, least / len(cuts), high / len(cuts)))
        factor_of = factor_of * jnp.repeat(draws, extent[axis_at] // shards_of).reshape([-1 if axis == axis_at else 1 for axis in range(len(extent))])
    return factor_of


def split_up(amount, total, limit, slope):
    portions = [(1 << 20) // math.isqrt(grade ** slope) + 1 for grade in range(2, amount + 1)]
    spare, given = total - limit - (amount - 1), [1] * (amount - 1)
    while spare > 0:
        movable = [i for i in range(amount - 1) if given[i] < limit]
        mass, left = sum([portions[i] for i in movable]), spare
        for i in movable:
            addition = min(limit - given[i], max(1, left * portions[i] // mass), spare)
            given[i] = given[i] + addition
            spare = spare - addition
    return np.array([limit] + given)


def ragged_sizes(own_key, count, total, most, slope):
    if count == 2:
        one = jax.random.randint(own_key, (), max(1, total - most), min(most, total - 1) + 1)
        return jnp.stack([one, total - one])
    lengths = jnp.asarray(split_up(count, total, most, slope), jnp.int32)
    pairs = (count - 1) // 2
    source_of, taker = lengths[1:1 + 2 * pairs:2], lengths[2:2 + 2 * pairs:2]
    room = jnp.minimum(source_of - 1, most - taker)
    moved = jax.random.randint(jax.random.fold_in(own_key, 1), (pairs,), 0, 1 << 20) % (room + 1)
    lengths = lengths.at[1:1 + 2 * pairs:2].set(source_of - moved).at[2:2 + 2 * pairs:2].set(taker + moved)
    return lengths[jax.random.permutation(jax.random.fold_in(own_key, 2), count)]


def gaussian(own_key, dims, spread, reach, shards=(), held_as=jnp.bfloat16):
    array = jax.random.normal(own_key, dims, jnp.float32) * spread
    if len(shards) > 0:
        array = block_levels(own_key, dims, shards, -0.22, 0.18) * array
    return jnp.clip(array, min=-reach, max=reach).astype(held_as)


def setup_inputs(seed: int = 0) -> dict:
    keys = jax.random.split(jax.random.key(seed), 6)
    queries = draw_queries(jax.random.fold_in(keys[5], 71), 0)
    new_kv = gaussian(keys[1], (NEW, KV * 2 * HD), 1.0, 5.0, ((0, 512),))
    cache_kv = draw_cache_kv(jax.random.fold_in(keys[5], 71), 0)
    hit_tokens = ragged_sizes(keys[3], N_CTX, HITS, CACHE_DEV, 2).astype(jnp.int32)
    block_order = jax.random.permutation(keys[4], N_CTX).astype(jnp.int32)
    return dict(queries=queries, new_kv=new_kv, cache_kv=cache_kv, hit_tokens=hit_tokens, block_order=block_order)


def reference(queries, new_kv, cache_kv, hit_tokens, block_order):
    group_size = HQ // KV
    score_scale = 1.0 / math.sqrt(HD)
    cache_index = jnp.arange(CACHE, dtype=jnp.int32)
    cache_live = cache_index % CACHE_DEV < hit_tokens[cache_index // CACHE_DEV]
    new_index = jnp.arange(NEW, dtype=jnp.int32)
    new_position = block_order[new_index // TOK_DEV] * TOK_DEV + new_index % TOK_DEV
    key_rows = jnp.concatenate([cache_kv, new_kv], axis=0).reshape(CACHE + NEW, KV, 2, HD)
    allowed = jnp.concatenate([jnp.broadcast_to(cache_live[None, :], (NEW, CACHE)), new_position[None, :] <= new_position[:, None]], axis=1)

    def one_head(head_index):
        kv_head = head_index // group_size
        chosen = lax.dynamic_index_in_dim(key_rows, kv_head, 1, keepdims=False)
        query_part = lax.dynamic_slice_in_dim(queries, head_index * HD, HD, 1)
        scores = jnp.dot(query_part, chosen[:, 0, :].T, preferred_element_type=jnp.float32) * score_scale
        scores = jnp.where(allowed, scores, -jnp.inf)
        weights = jnp.exp(scores - lax.optimization_barrier(jnp.max(scores, axis=1, keepdims=True)))
        weight_total = lax.optimization_barrier(jnp.sum(weights, axis=1, keepdims=True))
        blended = jnp.dot(weights.astype(jnp.bfloat16), chosen[:, 1, :], preferred_element_type=jnp.float32)
        return (blended / weight_total).astype(jnp.bfloat16)
    heads_out = lax.map(one_head, jnp.arange(HQ, dtype=jnp.int32))
    return heads_out.transpose(1, 0, 2).reshape(NEW, HQ * HD)
```

```python
import functools
import math

import jax
import jax.numpy as jnp
from jax import lax
from jax.experimental import pallas as pl
from jax.experimental.pallas import tpu as pltpu
from jax.sharding import PartitionSpec as P

HD = 128
MESH = pl.DeviceIdType.MESH
FLOOR = -1e30
SCALE = math.log2(math.e) / math.sqrt(HD)
ROUNDS = 16
TILE = 256
DEAD = 1e9


def kernel(q_ref, new_ref, cache_ref, meta_ref, o_ref, raw, kv, meta, qs, acc, top, tot,
           a2a_send, a2a_recv, meta_send, meta_recv, zs, ys, ss, rs):
    ctx, tp = lax.axis_index("ctx"), lax.axis_index("tp")
    lane, y = ctx // 4, ctx % 4
    x, half, core = tp // 4, (tp // 2) % 2, tp % 2
    quad, place = half * 2 + lane // 4, lane % 4
    next_quad = half * 2 + 1 - lane // 4

    def at(x_=None, y_=None, quad_=None, place_=None, core_=None):
        x_ = x if x_ is None else x_
        y_ = y if y_ is None else y_
        quad_ = quad if quad_ is None else quad_
        place_ = place if place_ is None else place_
        core_ = core if core_ is None else core_
        return (((quad_ % 2) * 4 + place_) * 4 + y_, x_ * 4 + (quad_ // 2) * 2 + core_)

    def off(value, d):
        return (value + d) % 4

    barrier = pltpu.get_barrier_semaphore()

    def greet(device):
        pl.semaphore_signal(barrier, inc=1, device_id=device, device_id_type=MESH)

    greet(at(quad_=3 - quad))
    for d in range(1, 4):
        greet(at(x_=off(x, d), quad_=3 - quad))
    greet(at(quad_=next_quad))
    for d in range(1, 4):
        greet(at(place_=off(place, d)))
        greet(at(x_=off(x, d)))
        greet(at(y_=off(y, d)))
    greet(at(core_=1 - core))

    raw[...] = jnp.concatenate([new_ref[...], cache_ref[...]], axis=0)
    meta[lane, pl.ds(y * 2, 2)] = meta_ref[...]
    for h in range(8):
        qs[h * 128:(h + 1) * 128] = q_ref[:, h * 128:(h + 1) * 128]
    acc[...] = jnp.zeros_like(acc)
    tot[...] = jnp.zeros_like(tot)
    top[...] = jnp.full_like(top, FLOOR)

    own_z = quad * 4 + place
    kv[own_z, core, y, x] = raw[:, pl.ds(pl.multiple_of((x * 2 + half) * 256, 256), 256)]

    pl.semaphore_wait(barrier, 15)

    def send(src, dst, s_sem, r_sem, device):
        return pltpu.make_async_remote_copy(src_ref=src, dst_ref=dst, send_sem=s_sem, recv_sem=r_sem,
                                            device_id=device, device_id_type=MESH)

    def piece(x_, half_):
        return raw.at[:, pl.ds(pl.multiple_of((x_ * 2 + half_) * 256, 256), 256)]

    def near_copy(d, x_from=None):
        x_from = x if x_from is None else x_from
        to = off(x, d)
        return send(piece(to, half), kv.at[own_z, core, y, x_from], a2a_send.at[d - 1], a2a_recv.at[d - 1], at(x_=to))

    def far_copy(d, arriving=False):
        to = off(x, d)
        z_from = (3 - quad) * 4 + place if arriving else own_z
        x_from = off(x, 4 - d) if arriving else x
        return send(piece(to, 1 - half), kv.at[z_from, core, y, x_from], a2a_send.at[d + 3], a2a_recv.at[d + 3], at(x_=to, quad_=3 - quad))

    def meta_y(d, row):
        rows = pl.ds(row * 2, 2)
        return send(meta.at[lane, rows], meta.at[lane, rows], meta_send.at[d - 1], meta_recv.at[d - 1], at(y_=off(y, d)))

    def meta_z(d, lane_, i):
        device = at(place_=off(place, d)) if d else at(quad_=next_quad)
        return send(meta.at[lane_], meta.at[lane_], meta_send.at[i], meta_recv.at[i], device)

    for d in range(1, 4):
        near_copy(d).start()
    for d in range(4):
        far_copy(d).start()
    for d in range(1, 4):
        meta_y(d, y).start()

    def unit(i):
        order = [(0, 0), (1, 0), (0, 1), (0, 2), (0, 3), (2, 0), (1, 1), (1, 2), (1, 3), (3, 0), (2, 1), (2, 2), (2, 3), (3, 1), (3, 2), (3, 3)]
        code = jnp.int32(order[0][0] * 4 + order[0][1])
        for n in range(1, ROUNDS):
            code = jnp.where(i == n, order[n][0] * 4 + order[n][1], code)
        kind, step = code // 4, code % 4
        from_quad = jnp.where(kind == 0, quad, jnp.where(kind == 1, 3 - quad, jnp.where(kind == 2, next_quad, 3 - next_quad)))
        return from_quad * 4 + off(place, step), kind, step

    def mate_copy(zz, d):
        ref = kv.at[zz, core, y]
        return send(ref, ref, zs.at[zz // 4, d], rs.at[zz, core, y], at(place_=off(place, d)))

    def quad_copy(zz):
        ref = kv.at[zz, core, y]
        return send(ref, ref, zs.at[zz // 4, 0], rs.at[zz, core, y], at(quad_=next_quad))

    def y_copy(zz, d):
        ref = kv.at[zz, core, y]
        return send(ref, ref, ys.at[zz, d - 1], rs.at[zz, core, y], at(y_=off(y, d)))

    def core_copy(zz, row):
        ref = kv.at[zz, core, row]
        return send(ref, ref, ss.at[zz, row], rs.at[zz, core, row], at(core_=1 - core))

    def arrival(zz, core_, row):
        ref = kv.at[zz, core_, row]
        return send(ref, ref, ss.at[zz, row], rs.at[zz, core_, row], at(core_=1 - core))

    def take_in(i):
        zz, kind, step = unit(i)

        @pl.when(i == 0)
        def _():
            for d in range(1, 4):
                near_copy(d, off(x, 4 - d)).wait_recv()

        @pl.when(i == 1)
        def _():
            for d in range(4):
                far_copy(d, True).wait_recv()

        @pl.when(i >= 2)
        def _():
            arrival(zz, core, y).wait_recv()

        @pl.when(jnp.logical_and(step == 0, kind < 2))
        def _():
            quad_copy(zz).start()

        @pl.when(step == 0)
        def _():
            for d in range(1, 4):
                mate_copy(zz, d).start()

        for d in (2, 1, 3):
            y_copy(zz, d).start()
        core_copy(zz, y).start()

    def along_y(i):
        zz, _, _ = unit(i)
        for d in (1, 3, 2):
            row = off(y, d)
            arrival(zz, core, row).wait_recv()
            core_copy(zz, row).start()

    own_block = meta_ref[1:2, :]
    number = lax.broadcasted_iota(jnp.int32, (1, 128), 1)
    token = lax.broadcasted_iota(jnp.int32, (128, 1), 0).astype(jnp.float32)
    query_position = own_block[:, 0:1] * 128.0 + token

    def key_positions(zz):
        lane_, half_ = zz % 8, zz // 8
        rows = meta[lane_]
        parts = []
        for part in range(4):
            core_, pair = part // 2, part % 2
            low = number < 64
            r = 4 * pair
            hits = jnp.where(low, rows[r:r + 1], rows[r + 2:r + 3])
            block = jnp.where(low, rows[r + 1:r + 2], rows[r + 3:r + 4])
            inner = number % 64
            slot = ((inner // 16) * 32 + half_ * 16 + core_ * 8 + inner % 8).astype(jnp.float32)
            cached = (inner // 8) % 2 == 1
            parts.append(jnp.where(cached, jnp.where(slot < hits, -1.0, DEAD), block * 128.0 + slot))
        return jnp.concatenate(parts, axis=1)

    def absorb(n):
        zz, _, _ = unit(n)
        for row in range(4):
            arrival(zz, 1 - core, row).wait_recv()
        block = kv[zz].reshape(512, 256)
        keys, values = block[:, :HD], block[:, HD:]
        allowed = key_positions(zz) <= query_position
        allowed = jnp.concatenate([allowed] * (TILE // 128), axis=0)

        def tile(t, carry):
            rows = pl.ds(pl.multiple_of(t * TILE, TILE), TILE)
            scores = lax.dot_general(qs[rows], keys, (((1,), (1,)), ((), ())), preferred_element_type=jnp.float32)
            scores = jnp.where(allowed, scores, FLOOR)
            pieces = [scores[:, i * 128:(i + 1) * 128] for i in range(4)]
            old = top[rows]
            new = jnp.maximum(old, jnp.max(functools.reduce(jnp.maximum, pieces), axis=1, keepdims=True))
            top[rows] = new
            factor = jnp.exp2((old - new) * SCALE)
            shift = new * SCALE
            weights = [jnp.exp2(piece * SCALE - shift) for piece in pieces]
            tot[rows] = tot[rows] * factor + functools.reduce(jnp.add, weights)
            rounded = jnp.concatenate([w.astype(jnp.bfloat16) for w in weights], axis=1)
            acc[rows] = acc[rows] * factor + jnp.dot(rounded, values, preferred_element_type=jnp.float32)
            return carry

        lax.fori_loop(0, 1024 // TILE, tile, 0)

    take_in(0)
    take_in(1)
    for d in range(1, 4):
        meta_y(d, off(y, 4 - d)).wait_recv()
    for d in range(4):
        meta_z(d, lane, 3 + d).start()
    next_lane = (next_quad % 2) * 4 + place
    meta_z(0, next_lane, 3).wait_recv()
    for d in range(1, 4):
        meta_z(d, next_lane, 6 + d).start()
    for d in range(1, 4):
        meta_z(d, (quad % 2) * 4 + off(place, 4 - d), 3 + d).wait_recv()
        meta_z(d, (next_quad % 2) * 4 + off(place, 4 - d), 6 + d).wait_recv()

    def rounds(n, carry):
        @pl.when(n < 7)
        def _():
            take_in(2 + 2 * n)
            take_in(3 + 2 * n)

        along_y(n)

        @pl.when(n >= 1)
        def _():
            absorb(n - 1)
        return carry

    lax.fori_loop(0, ROUNDS, rounds, 0)
    absorb(ROUNDS - 1)

    for h in range(8):
        rows = slice(h * 128, (h + 1) * 128)
        total = jnp.sum(tot[rows], axis=1, keepdims=True)
        o_ref[:, rows] = (acc[rows] / total).astype(jnp.bfloat16)

    for d in range(1, 4):
        near_copy(d).wait_send()
        meta_y(d, y).wait_send()
        meta_z(d, next_lane, 6 + d).wait_send()
    for d in range(4):
        far_copy(d).wait_send()
        meta_z(d, lane, 3 + d).wait_send()
    quad_copy(own_z).wait_send()
    quad_copy((3 - quad) * 4 + place).wait_send()

    def drain(n, carry):
        for d in range(1, 4):
            y_copy(n, d).wait_send()
        for row in range(4):
            core_copy(n, row).wait_send()
        return carry

    def drain_quads(n, carry):
        for d in range(1, 4):
            mate_copy(n * 4 + place, d).wait_send()
        return carry

    lax.fori_loop(0, ROUNDS, drain, 0)
    lax.fori_loop(0, 4, drain_quads, 0)


def local(queries, new_kv, cache_kv, hit_tokens, block_order):
    facts = jnp.broadcast_to(jnp.concatenate([hit_tokens, block_order])[:, None].astype(jnp.float32), (2, 128))
    vmem = pl.BlockSpec(memory_space=pltpu.VMEM)
    dma = pltpu.SemaphoreType.DMA
    return pl.pallas_call(
        kernel,
        out_shape=jax.ShapeDtypeStruct(queries.shape, jnp.bfloat16),
        in_specs=[vmem] * 4,
        out_specs=vmem,
        scratch_shapes=[
            pltpu.VMEM((16, 2048), jnp.bfloat16),
            pltpu.VMEM((16, 2, 4, 4, 16, 256), jnp.bfloat16),
            pltpu.VMEM((8, 8, 128), jnp.float32),
            pltpu.VMEM((1024, 128), jnp.bfloat16),
            pltpu.VMEM((1024, 128), jnp.float32),
            pltpu.VMEM((1024, 128), jnp.float32),
            pltpu.VMEM((1024, 128), jnp.float32),
            dma((7,)), dma((7,)), dma((10,)), dma((10,)),
            dma((4, 4)), dma((16, 3)), dma((16, 4)), dma((16, 2, 4)),
        ],
        compiler_params=pltpu.CompilerParams(collective_id=0, has_side_effects=True, vmem_limit_bytes=48 * 1024 * 1024),
        cost_estimate=pl.CostEstimate(flops=4 * 1024 * 8192 * 128, bytes_accessed=1 << 20, transcendentals=1024 * 8192),
    )(queries, new_kv, cache_kv, facts)


def solution(mesh):
    in_specs = (P("ctx", "tp"), P(("ctx", "tp"), None), P(("ctx", "tp"), None), P("ctx"), P("ctx"))
    return jax.shard_map(local, mesh=mesh, in_specs=in_specs, out_specs=P("ctx", "tp"), check_vma=False)
```

```python
import functools
import math

import jax
import jax.numpy as jnp
from jax import lax
from jax.experimental import pallas as pl
from jax.experimental.pallas import tpu as pltpu
from jax.sharding import PartitionSpec as P

HD = 128
MESH = pl.DeviceIdType.MESH
FLOOR = -1e30
SCALE = math.log2(math.e) / math.sqrt(HD)
ROUNDS = 16
TILE = 1024
DEAD = 1e9


def kernel(q_ref, new_ref, cache_ref, hits_ref, block_ref, o_ref, new_rows, cache_rows, hits, block, raw, kv, meta, qs, acc, top, tot,
           load_sem, a2a_send, a2a_recv, meta_send, meta_recv, zs, ys, ss, rs):
    ctx, tp = lax.axis_index("ctx"), lax.axis_index("tp")
    lane, y = ctx // 4, ctx % 4
    x, half, core = tp // 4, (tp // 2) % 2, tp % 2
    quad, place = half * 2 + lane // 4, lane % 4
    next_quad = half * 2 + 1 - lane // 4

    def at(x_=None, y_=None, quad_=None, place_=None, core_=None):
        x_ = x if x_ is None else x_
        y_ = y if y_ is None else y_
        quad_ = quad if quad_ is None else quad_
        place_ = place if place_ is None else place_
        core_ = core if core_ is None else core_
        return (((quad_ % 2) * 4 + place_) * 4 + y_, x_ * 4 + (quad_ // 2) * 2 + core_)

    def off(value, d):
        return (value + d) % 4

    barrier = pltpu.get_barrier_semaphore()

    def greet(device):
        pl.semaphore_signal(barrier, inc=1, device_id=device, device_id_type=MESH)

    greet(at(quad_=3 - quad))
    for d in range(1, 4):
        greet(at(x_=off(x, d), quad_=3 - quad))
    greet(at(quad_=next_quad))
    for d in range(1, 4):
        greet(at(place_=off(place, d)))
        greet(at(x_=off(x, d)))
        greet(at(y_=off(y, d)))
    greet(at(core_=1 - core))

    loads = [
        pltpu.make_async_copy(new_ref, new_rows, load_sem.at[0]),
        pltpu.make_async_copy(cache_ref, cache_rows, load_sem.at[1]),
        pltpu.make_async_copy(hits_ref, hits, load_sem.at[2]),
        pltpu.make_async_copy(block_ref, block, load_sem.at[3]),
    ] + [pltpu.make_async_copy(q_ref.at[:, h * 128:(h + 1) * 128], qs.at[h * 128:(h + 1) * 128], load_sem.at[4 + h]) for h in range(8)]
    for load in loads:
        load.start()
    acc[...] = jnp.zeros_like(acc)
    tot[...] = jnp.zeros_like(tot)
    top[...] = jnp.full_like(top, FLOOR)
    for load in loads:
        load.wait()

    raw[...] = jnp.concatenate([new_rows[...], cache_rows[...]], axis=0)
    own_block = block[0].astype(jnp.float32)
    is_hits = lax.broadcasted_iota(jnp.int32, (2, 128), 0) == 0
    meta[lane, pl.ds(y * 2, 2)] = jnp.where(is_hits, hits[0].astype(jnp.float32), own_block)
    own_z = quad * 4 + place
    kv[own_z, core, y, x] = raw[:, pl.ds(pl.multiple_of((x * 2 + half) * 256, 256), 256)]

    pl.semaphore_wait(barrier, 15)

    def send(src, dst, s_sem, r_sem, device):
        return pltpu.make_async_remote_copy(src_ref=src, dst_ref=dst, send_sem=s_sem, recv_sem=r_sem,
                                            device_id=device, device_id_type=MESH)

    def piece(x_, half_):
        return raw.at[:, pl.ds(pl.multiple_of((x_ * 2 + half_) * 256, 256), 256)]

    def near_copy(d, x_from=None):
        x_from = x if x_from is None else x_from
        to = off(x, d)
        return send(piece(to, half), kv.at[own_z, core, y, x_from], a2a_send.at[d - 1], a2a_recv.at[d - 1], at(x_=to))

    def far_copy(d, arriving=False):
        to = off(x, d)
        z_from = (3 - quad) * 4 + place if arriving else own_z
        x_from = off(x, 4 - d) if arriving else x
        return send(piece(to, 1 - half), kv.at[z_from, core, y, x_from], a2a_send.at[d + 3], a2a_recv.at[d + 3], at(x_=to, quad_=3 - quad))

    def meta_y(d, row):
        rows = pl.ds(row * 2, 2)
        return send(meta.at[lane, rows], meta.at[lane, rows], meta_send.at[d - 1], meta_recv.at[d - 1], at(y_=off(y, d)))

    def meta_z(d, lane_, i):
        device = at(place_=off(place, d)) if d else at(quad_=next_quad)
        return send(meta.at[lane_], meta.at[lane_], meta_send.at[i], meta_recv.at[i], device)

    for d in range(1, 4):
        near_copy(d).start()
    for d in range(4):
        far_copy(d).start()
    for d in range(1, 4):
        meta_y(d, y).start()

    def unit(i):
        order = [(0, 0), (1, 0), (0, 1), (0, 2), (0, 3), (2, 0), (1, 1), (1, 2), (1, 3), (3, 0), (2, 1), (2, 2), (2, 3), (3, 1), (3, 2), (3, 3)]
        code = jnp.int32(order[0][0] * 4 + order[0][1])
        for n in range(1, ROUNDS):
            code = jnp.where(i == n, order[n][0] * 4 + order[n][1], code)
        kind, step = code // 4, code % 4
        from_quad = jnp.where(kind == 0, quad, jnp.where(kind == 1, 3 - quad, jnp.where(kind == 2, next_quad, 3 - next_quad)))
        return from_quad * 4 + off(place, step), kind, step

    def mate_copy(zz, d):
        ref = kv.at[zz, core, y]
        return send(ref, ref, zs.at[zz // 4, d], rs.at[zz, core, y], at(place_=off(place, d)))

    def quad_copy(zz):
        ref = kv.at[zz, core, y]
        return send(ref, ref, zs.at[zz // 4, 0], rs.at[zz, core, y], at(quad_=next_quad))

    def y_copy(zz, d):
        ref = kv.at[zz, core, y]
        return send(ref, ref, ys.at[zz, d - 1], rs.at[zz, core, y], at(y_=off(y, d)))

    def core_copy(zz, row):
        ref = kv.at[zz, core, row]
        return send(ref, ref, ss.at[zz, row], rs.at[zz, core, row], at(core_=1 - core))

    def arrival(zz, core_, row):
        ref = kv.at[zz, core_, row]
        return send(ref, ref, ss.at[zz, row], rs.at[zz, core_, row], at(core_=1 - core))

    def take_in(i):
        zz, kind, step = unit(i)

        @pl.when(i == 0)
        def _():
            for d in range(1, 4):
                near_copy(d, off(x, 4 - d)).wait_recv()

        @pl.when(i == 1)
        def _():
            for d in range(4):
                far_copy(d, True).wait_recv()

        @pl.when(i >= 2)
        def _():
            arrival(zz, core, y).wait_recv()

        @pl.when(jnp.logical_and(step == 0, kind < 2))
        def _():
            quad_copy(zz).start()

        @pl.when(step == 0)
        def _():
            for d in range(1, 4):
                mate_copy(zz, d).start()

        for d in (2, 1, 3):
            y_copy(zz, d).start()
        core_copy(zz, y).start()

    def along_y(i):
        zz, _, _ = unit(i)
        for d in (1, 3, 2):
            row = off(y, d)
            arrival(zz, core, row).wait_recv()
            core_copy(zz, row).start()

    number = lax.broadcasted_iota(jnp.int32, (1, 128), 1)
    token = lax.broadcasted_iota(jnp.int32, (128, 1), 0).astype(jnp.float32)
    query_position = own_block * 128.0 + token

    def key_positions(zz):
        lane_, half_ = zz % 8, zz // 8
        rows = meta[lane_]
        parts = []
        for part in range(4):
            core_, pair = part // 2, part % 2
            low = number < 64
            r = 4 * pair
            hits = jnp.where(low, rows[r:r + 1], rows[r + 2:r + 3])
            block = jnp.where(low, rows[r + 1:r + 2], rows[r + 3:r + 4])
            inner = number % 64
            slot = ((inner // 16) * 32 + half_ * 16 + core_ * 8 + inner % 8).astype(jnp.float32)
            cached = (inner // 8) % 2 == 1
            parts.append(jnp.where(cached, jnp.where(slot < hits, -1.0, DEAD), block * 128.0 + slot))
        return jnp.concatenate(parts, axis=1)

    def absorb(n):
        zz, _, _ = unit(n)
        for row in range(4):
            arrival(zz, 1 - core, row).wait_recv()
        block = kv[zz].reshape(512, 256)
        keys, values = block[:, :HD], block[:, HD:]
        allowed = key_positions(zz) <= query_position
        allowed = jnp.concatenate([allowed] * (TILE // 128), axis=0)

        def tile(t, carry):
            rows = pl.ds(pl.multiple_of(t * TILE, TILE), TILE)
            scores = lax.dot_general(qs[rows], keys, (((1,), (1,)), ((), ())), preferred_element_type=jnp.float32)
            scores = jnp.where(allowed, scores, FLOOR)
            pieces = [scores[:, i * 128:(i + 1) * 128] for i in range(4)]
            old = top[rows]
            new = jnp.maximum(old, jnp.max(functools.reduce(jnp.maximum, pieces), axis=1, keepdims=True))
            top[rows] = new
            factor = jnp.exp2((old - new) * SCALE)
            shift = new * SCALE
            weights = [jnp.exp2(piece * SCALE - shift) for piece in pieces]
            tot[rows] = tot[rows] * factor + functools.reduce(jnp.add, weights)
            rounded = jnp.concatenate([w.astype(jnp.bfloat16) for w in weights], axis=1)
            acc[rows] = acc[rows] * factor + jnp.dot(rounded, values, preferred_element_type=jnp.float32)
            return carry

        lax.fori_loop(0, 1024 // TILE, tile, 0)

    def take_in_from(first, last):
        lax.fori_loop(first, last, lambda i, carry: (take_in(i), carry)[1], 0)

    next_lane = (next_quad % 2) * 4 + place
    take_in_from(0, 6)
    for d in range(1, 4):
        meta_y(d, off(y, 4 - d)).wait_recv()
    for d in range(4):
        meta_z(d, lane, 3 + d).start()
    along_y(0)
    take_in_from(6, 10)
    meta_z(0, next_lane, 3).wait_recv()
    for d in range(1, 4):
        meta_z(d, next_lane, 6 + d).start()
    along_y(1)
    for d in range(1, 4):
        meta_z(d, (quad % 2) * 4 + off(place, 4 - d), 3 + d).wait_recv()
        meta_z(d, (next_quad % 2) * 4 + off(place, 4 - d), 6 + d).wait_recv()

    def rounds(n, carry):
        @pl.when(n < 6)
        def _():
            take_in(n + 10)

        @pl.when(n < ROUNDS - 2)
        def _():
            along_y(n + 2)

        absorb(n)
        return carry

    lax.fori_loop(0, ROUNDS, rounds, 0)

    for h in range(8):
        rows = slice(h * 128, (h + 1) * 128)
        total = jnp.sum(tot[rows], axis=1, keepdims=True)
        o_ref[:, rows] = (acc[rows] / total).astype(jnp.bfloat16)

    for d in range(1, 4):
        near_copy(d).wait_send()
        meta_y(d, y).wait_send()
        meta_z(d, next_lane, 6 + d).wait_send()
    for d in range(4):
        far_copy(d).wait_send()
        meta_z(d, lane, 3 + d).wait_send()
    quad_copy(own_z).wait_send()
    quad_copy((3 - quad) * 4 + place).wait_send()

    def drain(n, carry):
        for d in range(1, 4):
            y_copy(n, d).wait_send()
        for row in range(4):
            core_copy(n, row).wait_send()
        return carry

    def drain_quads(n, carry):
        for d in range(1, 4):
            mate_copy(n * 4 + place, d).wait_send()
        return carry

    lax.fori_loop(0, ROUNDS, drain, 0)
    lax.fori_loop(0, 4, drain_quads, 0)


def local(queries, new_kv, cache_kv, hit_tokens, block_order):
    dma = pltpu.SemaphoreType.DMA
    return pl.pallas_call(
        kernel,
        out_shape=jax.ShapeDtypeStruct(queries.shape, jnp.bfloat16),
        in_specs=[pl.BlockSpec(memory_space=pltpu.HBM)] * 5,
        out_specs=pl.BlockSpec(memory_space=pltpu.VMEM),
        scratch_shapes=[
            pltpu.VMEM((8, 2048), jnp.bfloat16),
            pltpu.VMEM((8, 2048), jnp.bfloat16),
            pltpu.SMEM((1,), jnp.int32),
            pltpu.SMEM((1,), jnp.int32),
            pltpu.VMEM((16, 2048), jnp.bfloat16),
            pltpu.VMEM((16, 2, 4, 4, 16, 256), jnp.bfloat16),
            pltpu.VMEM((8, 8, 128), jnp.float32),
            pltpu.VMEM((1024, 128), jnp.bfloat16),
            pltpu.VMEM((1024, 128), jnp.float32),
            pltpu.VMEM((1024, 128), jnp.float32),
            pltpu.VMEM((1024, 128), jnp.float32),
            dma((12,)), dma((7,)), dma((7,)), dma((10,)), dma((10,)),
            dma((4, 4)), dma((16, 3)), dma((16, 4)), dma((16, 2, 4)),
        ],
        compiler_params=pltpu.CompilerParams(collective_id=0, has_side_effects=True, vmem_limit_bytes=48 * 1024 * 1024),
        cost_estimate=pl.CostEstimate(flops=4 * 1024 * 8192 * 128, bytes_accessed=1 << 20, transcendentals=1024 * 8192),
    )(queries, new_kv, cache_kv, hit_tokens, block_order)


def solution(mesh):
    in_specs = (P("ctx", "tp"), P(("ctx", "tp"), None), P(("ctx", "tp"), None), P("ctx"), P("ctx"))
    return jax.shard_map(local, mesh=mesh, in_specs=in_specs, out_specs=P("ctx", "tp"), check_vma=False)
```

```python
import functools
import math

import jax
import jax.numpy as jnp
from jax import lax
from jax.experimental import pallas as pl
from jax.experimental.pallas import tpu as pltpu
from jax.sharding import PartitionSpec as P

HD = 128
MESH = pl.DeviceIdType.MESH
FLOOR = -1e30
SCALE = math.log2(math.e) / math.sqrt(HD)
ROUNDS = 16
TILE = 1024
DEAD = 1e9


def kernel(q_ref, new_ref, cache_ref, hits_ref, block_ref, o_ref, new_rows, cache_rows, hits, block, raw, kv, meta, qs, acc, top, tot,
           load_sem, a2a_send, a2a_recv, meta_send, meta_recv, zs, ys, ss, z_recv, y_recv, core_recv):
    ctx, tp = lax.axis_index("ctx"), lax.axis_index("tp")
    lane, y = ctx // 4, ctx % 4
    x, half, core = tp // 4, (tp // 2) % 2, tp % 2
    quad, place = half * 2 + lane // 4, lane % 4
    next_quad = half * 2 + 1 - lane // 4

    def at(x_=None, y_=None, quad_=None, place_=None, core_=None):
        x_ = x if x_ is None else x_
        y_ = y if y_ is None else y_
        quad_ = quad if quad_ is None else quad_
        place_ = place if place_ is None else place_
        core_ = core if core_ is None else core_
        return (((quad_ % 2) * 4 + place_) * 4 + y_, x_ * 4 + (quad_ // 2) * 2 + core_)

    def off(value, d):
        return (value + d) % 4

    barrier = pltpu.get_barrier_semaphore()

    def greet(device):
        pl.semaphore_signal(barrier, inc=1, device_id=device, device_id_type=MESH)

    greet(at(quad_=3 - quad))
    for d in range(1, 4):
        greet(at(x_=off(x, d), quad_=3 - quad))
    greet(at(quad_=next_quad))
    for d in range(1, 4):
        greet(at(place_=off(place, d)))
        greet(at(x_=off(x, d)))
        greet(at(y_=off(y, d)))
    greet(at(core_=1 - core))

    loads = [
        pltpu.make_async_copy(new_ref, new_rows, load_sem.at[0]),
        pltpu.make_async_copy(cache_ref, cache_rows, load_sem.at[1]),
        pltpu.make_async_copy(hits_ref, hits, load_sem.at[2]),
        pltpu.make_async_copy(block_ref, block, load_sem.at[3]),
    ] + [pltpu.make_async_copy(q_ref.at[:, h * 128:(h + 1) * 128], qs.at[h * 128:(h + 1) * 128], load_sem.at[4 + h]) for h in range(8)]
    for load in loads:
        load.start()
    acc[...] = jnp.zeros_like(acc)
    tot[...] = jnp.zeros_like(tot)
    top[...] = jnp.full_like(top, FLOOR)
    for load in loads:
        load.wait()

    raw[...] = jnp.concatenate([new_rows[...], cache_rows[...]], axis=0)
    own_block = block[0].astype(jnp.float32)
    is_hits = lax.broadcasted_iota(jnp.int32, (2, 128), 0) == 0
    meta[lane, pl.ds(y * 2, 2)] = jnp.where(is_hits, hits[0].astype(jnp.float32), own_block)
    own_z = quad * 4 + place
    kv[own_z, core, y, x] = raw[:, pl.ds(pl.multiple_of((x * 2 + half) * 256, 256), 256)]

    pl.semaphore_wait(barrier, 15)

    def send(src, dst, s_sem, r_sem, device):
        return pltpu.make_async_remote_copy(src_ref=src, dst_ref=dst, send_sem=s_sem, recv_sem=r_sem,
                                            device_id=device, device_id_type=MESH)

    def piece(x_, half_):
        return raw.at[:, pl.ds(pl.multiple_of((x_ * 2 + half_) * 256, 256), 256)]

    def near_copy(d, x_from=None):
        x_from = x if x_from is None else x_from
        to = off(x, d)
        return send(piece(to, half), kv.at[own_z, core, y, x_from], a2a_send.at[d - 1], a2a_recv.at[d - 1], at(x_=to))

    def far_copy(d, arriving=False):
        to = off(x, d)
        z_from = (3 - quad) * 4 + place if arriving else own_z
        x_from = off(x, 4 - d) if arriving else x
        return send(piece(to, 1 - half), kv.at[z_from, core, y, x_from], a2a_send.at[d + 3], a2a_recv.at[d + 3], at(x_=to, quad_=3 - quad))

    def meta_y(d, row):
        rows = pl.ds(row * 2, 2)
        return send(meta.at[lane, rows], meta.at[lane, rows], meta_send.at[d - 1], meta_recv.at[d - 1], at(y_=off(y, d)))

    def meta_z(d, lane_, i):
        device = at(place_=off(place, d)) if d else at(quad_=next_quad)
        return send(meta.at[lane_], meta.at[lane_], meta_send.at[i], meta_recv.at[i], device)

    for d in range(1, 4):
        near_copy(d).start()
    for d in range(4):
        far_copy(d).start()
    for d in range(1, 4):
        meta_y(d, y).start()

    def unit(i):
        order = [(0, 0), (1, 0), (0, 1), (0, 2), (0, 3), (2, 0), (1, 1), (1, 2), (1, 3), (3, 0), (2, 1), (2, 2), (2, 3), (3, 1), (3, 2), (3, 3)]
        code = jnp.int32(order[0][0] * 4 + order[0][1])
        for n in range(1, ROUNDS):
            code = jnp.where(i == n, order[n][0] * 4 + order[n][1], code)
        kind, step = code // 4, code % 4
        from_quad = jnp.where(kind == 0, quad, jnp.where(kind == 1, 3 - quad, jnp.where(kind == 2, next_quad, 3 - next_quad)))
        return from_quad * 4 + off(place, step), kind, step

    def mate_copy(zz, d):
        ref = kv.at[zz, core, y]
        return send(ref, ref, zs, z_recv.at[zz], at(place_=off(place, d)))

    def quad_copy(zz):
        ref = kv.at[zz, core, y]
        return send(ref, ref, zs, z_recv.at[zz], at(quad_=next_quad))

    def y_copy(zz, d):
        ref = kv.at[zz, core, y]
        return send(ref, ref, ys, y_recv.at[zz], at(y_=off(y, d)))

    def core_copy(zz):
        ref = kv.at[zz, core]
        return send(ref, ref, ss, core_recv.at[zz], at(core_=1 - core))

    def await_bytes(ref, semaphore):
        pltpu.make_async_copy(ref, ref, semaphore).wait()

    def take_in(i):
        zz, kind, step = unit(i)

        @pl.when(i == 0)
        def _():
            for d in range(1, 4):
                near_copy(d, off(x, 4 - d)).wait_recv()

        @pl.when(i == 1)
        def _():
            for d in range(4):
                far_copy(d, True).wait_recv()

        @pl.when(i >= 2)
        def _():
            await_bytes(kv.at[zz, core, y], z_recv.at[zz])

        @pl.when(jnp.logical_and(step == 0, kind < 2))
        def _():
            quad_copy(zz).start()

        @pl.when(step == 0)
        def _():
            for d in range(1, 4):
                mate_copy(zz, d).start()

        for d in (2, 1, 3):
            y_copy(zz, d).start()

    def along_y(i):
        zz, _, _ = unit(i)
        await_bytes(kv.at[zz, core, 0:3], y_recv.at[zz])
        core_copy(zz).start()

    number = lax.broadcasted_iota(jnp.int32, (1, 128), 1)
    token = lax.broadcasted_iota(jnp.int32, (128, 1), 0).astype(jnp.float32)
    query_position = own_block * 128.0 + token

    def key_positions(zz):
        lane_, half_ = zz % 8, zz // 8
        rows = meta[lane_]
        parts = []
        for part in range(4):
            core_, pair = part // 2, part % 2
            low = number < 64
            r = 4 * pair
            hits = jnp.where(low, rows[r:r + 1], rows[r + 2:r + 3])
            block = jnp.where(low, rows[r + 1:r + 2], rows[r + 3:r + 4])
            inner = number % 64
            slot = ((inner // 16) * 32 + half_ * 16 + core_ * 8 + inner % 8).astype(jnp.float32)
            cached = (inner // 8) % 2 == 1
            parts.append(jnp.where(cached, jnp.where(slot < hits, -1.0, DEAD), block * 128.0 + slot))
        return jnp.concatenate(parts, axis=1)

    def absorb(n):
        zz, _, _ = unit(n)
        await_bytes(kv.at[zz, 1 - core], core_recv.at[zz])
        block = kv[zz].reshape(512, 256)
        keys, values = block[:, :HD], block[:, HD:]
        allowed = key_positions(zz) <= query_position
        allowed = jnp.concatenate([allowed] * (TILE // 128), axis=0)

        def tile(t, carry):
            rows = pl.ds(pl.multiple_of(t * TILE, TILE), TILE)
            scores = lax.dot_general(qs[rows], keys, (((1,), (1,)), ((), ())), preferred_element_type=jnp.float32)
            scores = jnp.where(allowed, scores, FLOOR)
            pieces = [scores[:, i * 128:(i + 1) * 128] for i in range(4)]
            old = top[rows]
            new = jnp.maximum(old, jnp.max(functools.reduce(jnp.maximum, pieces), axis=1, keepdims=True))
            top[rows] = new
            factor = jnp.exp2((old - new) * SCALE)
            shift = new * SCALE
            weights = [jnp.exp2(piece * SCALE - shift) for piece in pieces]
            tot[rows] = tot[rows] * factor + functools.reduce(jnp.add, weights)
            rounded = jnp.concatenate([w.astype(jnp.bfloat16) for w in weights], axis=1)
            acc[rows] = acc[rows] * factor + jnp.dot(rounded, values, preferred_element_type=jnp.float32)
            return carry

        lax.fori_loop(0, 1024 // TILE, tile, 0)

    def pick(n, table):
        value = jnp.int32(table[0])
        for i in range(1, len(table)):
            if table[i] != table[i - 1]:
                value = jnp.where(n >= i, table[i], value)
        return value

    def take_in_from(first, last):
        lax.fori_loop(first, last, lambda i, carry: (take_in(i), carry)[1], 0)

    def along_y_from(first, last):
        lax.fori_loop(first, last, lambda i, carry: (along_y(i), carry)[1], 0)

    taken = [6, 10, 11, 12, 13, 14, 15, 16, 16, 16, 16, 16, 16, 16, 16, 16, 16]
    moved = [2, 3, 4, 5, 6, 7, 8, 9, 10, 11, 12, 13, 14, 15, 16, 16, 16]
    next_lane = (next_quad % 2) * 4 + place
    take_in_from(0, taken[0])
    for d in range(1, 4):
        meta_y(d, off(y, 4 - d)).wait_recv()
    for d in range(4):
        meta_z(d, lane, 3 + d).start()
    along_y_from(0, moved[0])
    meta_z(0, next_lane, 3).wait_recv()
    for d in range(1, 4):
        meta_z(d, next_lane, 6 + d).start()

    def rounds(n, carry):
        take_in_from(pick(n, taken), pick(n + 1, taken))
        along_y_from(pick(n, moved), pick(n + 1, moved))

        @pl.when(n == 2)
        def _():
            for d in range(1, 4):
                meta_z(d, (quad % 2) * 4 + off(place, 4 - d), 3 + d).wait_recv()
                meta_z(d, (next_quad % 2) * 4 + off(place, 4 - d), 6 + d).wait_recv()

        absorb(n)
        return carry

    lax.fori_loop(0, ROUNDS, rounds, 0)

    for h in range(8):
        rows = slice(h * 128, (h + 1) * 128)
        total = jnp.sum(tot[rows], axis=1, keepdims=True)
        o_ref[:, rows] = (acc[rows] / total).astype(jnp.bfloat16)

    for d in range(1, 4):
        near_copy(d).wait_send()
        meta_y(d, y).wait_send()
        meta_z(d, next_lane, 6 + d).wait_send()
    for d in range(4):
        far_copy(d).wait_send()
        meta_z(d, lane, 3 + d).wait_send()
    await_bytes(kv.at[0:7, 0, 0:2], zs)
    await_bytes(kv.at[0:12, 0], ys)
    await_bytes(kv.at[:, 0], ss)


def local(queries, new_kv, cache_kv, hit_tokens, block_order):
    dma = pltpu.SemaphoreType.DMA
    return pl.pallas_call(
        kernel,
        out_shape=jax.ShapeDtypeStruct(queries.shape, jnp.bfloat16),
        in_specs=[pl.BlockSpec(memory_space=pltpu.HBM)] * 5,
        out_specs=pl.BlockSpec(memory_space=pltpu.VMEM),
        scratch_shapes=[
            pltpu.VMEM((8, 2048), jnp.bfloat16),
            pltpu.VMEM((8, 2048), jnp.bfloat16),
            pltpu.SMEM((1,), jnp.int32),
            pltpu.SMEM((1,), jnp.int32),
            pltpu.VMEM((16, 2048), jnp.bfloat16),
            pltpu.VMEM((16, 2, 4, 4, 16, 256), jnp.bfloat16),
            pltpu.VMEM((8, 8, 128), jnp.float32),
            pltpu.VMEM((1024, 128), jnp.bfloat16),
            pltpu.VMEM((1024, 128), jnp.float32),
            pltpu.VMEM((1024, 128), jnp.float32),
            pltpu.VMEM((1024, 128), jnp.float32),
            dma((12,)), dma((7,)), dma((7,)), dma((10,)), dma((10,)),
            dma, dma, dma, dma((16,)), dma((16,)), dma((16,)),
        ],
        compiler_params=pltpu.CompilerParams(collective_id=0, has_side_effects=True, vmem_limit_bytes=48 * 1024 * 1024),
        cost_estimate=pl.CostEstimate(flops=4 * 1024 * 8192 * 128, bytes_accessed=1 << 20, transcendentals=1024 * 8192),
    )(queries, new_kv, cache_kv, hit_tokens, block_order)


def solution(mesh):
    in_specs = (P("ctx", "tp"), P(("ctx", "tp"), None), P(("ctx", "tp"), None), P("ctx"), P("ctx"))
    return jax.shard_map(local, mesh=mesh, in_specs=in_specs, out_specs=P("ctx", "tp"), check_vma=False)
```

```python
import functools
import math

import jax
import jax.numpy as jnp
from jax import lax
from jax.experimental import pallas as pl
from jax.experimental.pallas import tpu as pltpu
from jax.sharding import PartitionSpec as P

HD = 128
MESH = pl.DeviceIdType.MESH
FLOOR = -1e30
SCALE = math.log2(math.e) / math.sqrt(HD)
ROUNDS = 16
TILE = 1024
DEAD = 1e9


def kernel(q_ref, new_ref, cache_ref, hits_ref, block_ref, o_ref, new_rows, cache_rows, hits, block, raw, kv, meta, qs, acc, top, tot,
           load_sem, a2a_send, a2a_recv, meta_send, meta_recv, zs, ys, ss, z_recv, y_recv, core_recv):
    ctx, tp = lax.axis_index("ctx"), lax.axis_index("tp")
    lane, y = ctx // 4, ctx % 4
    x, half, core = tp // 4, (tp // 2) % 2, tp % 2
    quad, place = half * 2 + lane // 4, lane % 4
    next_quad = half * 2 + 1 - lane // 4

    def at(x_=None, y_=None, quad_=None, place_=None, core_=None):
        x_ = x if x_ is None else x_
        y_ = y if y_ is None else y_
        quad_ = quad if quad_ is None else quad_
        place_ = place if place_ is None else place_
        core_ = core if core_ is None else core_
        return (((quad_ % 2) * 4 + place_) * 4 + y_, x_ * 4 + (quad_ // 2) * 2 + core_)

    def off(value, d):
        return (value + d) % 4

    barrier = pltpu.get_barrier_semaphore()

    def greet(device):
        pl.semaphore_signal(barrier, inc=1, device_id=device, device_id_type=MESH)

    greet(at(quad_=3 - quad))
    for d in range(1, 4):
        greet(at(x_=off(x, d), quad_=3 - quad))
    greet(at(quad_=next_quad))
    for d in range(1, 4):
        greet(at(place_=off(place, d)))
        greet(at(x_=off(x, d)))
        greet(at(y_=off(y, d)))
    greet(at(core_=1 - core))

    loads = [
        pltpu.make_async_copy(new_ref, new_rows, load_sem.at[0]),
        pltpu.make_async_copy(cache_ref, cache_rows, load_sem.at[1]),
        pltpu.make_async_copy(hits_ref, hits, load_sem.at[2]),
        pltpu.make_async_copy(block_ref, block, load_sem.at[3]),
    ] + [pltpu.make_async_copy(q_ref.at[:, h * 128:(h + 1) * 128], qs.at[h * 128:(h + 1) * 128], load_sem.at[4 + h]) for h in range(8)]
    for load in loads:
        load.start()
    acc[...] = jnp.zeros_like(acc)
    tot[...] = jnp.zeros_like(tot)
    top[...] = jnp.full_like(top, FLOOR)
    for load in loads:
        load.wait()

    raw[...] = jnp.concatenate([new_rows[...], cache_rows[...]], axis=0)
    own_block = block[0].astype(jnp.float32)
    is_hits = lax.broadcasted_iota(jnp.int32, (2, 128), 0) == 0
    meta[lane, pl.ds(y * 2, 2)] = jnp.where(is_hits, hits[0].astype(jnp.float32), own_block)
    own_z = quad * 4 + place
    kv[own_z, core, y, x] = raw[:, pl.ds(pl.multiple_of((x * 2 + half) * 256, 256), 256)]

    pl.semaphore_wait(barrier, 15)

    def send(src, dst, s_sem, r_sem, device):
        return pltpu.make_async_remote_copy(src_ref=src, dst_ref=dst, send_sem=s_sem, recv_sem=r_sem,
                                            device_id=device, device_id_type=MESH)

    def piece(x_, half_):
        return raw.at[:, pl.ds(pl.multiple_of((x_ * 2 + half_) * 256, 256), 256)]

    def near_copy(d, x_from=None):
        x_from = x if x_from is None else x_from
        to = off(x, d)
        return send(piece(to, half), kv.at[own_z, core, y, x_from], a2a_send.at[d - 1], a2a_recv.at[d - 1], at(x_=to))

    def far_copy(d, arriving=False):
        to = off(x, d)
        z_from = (3 - quad) * 4 + place if arriving else own_z
        x_from = off(x, 4 - d) if arriving else x
        return send(piece(to, 1 - half), kv.at[z_from, core, y, x_from], a2a_send.at[d + 3], a2a_recv.at[d + 3], at(x_=to, quad_=3 - quad))

    def meta_y(d, row):
        rows = pl.ds(row * 2, 2)
        return send(meta.at[lane, rows], meta.at[lane, rows], meta_send.at[d - 1], meta_recv.at[d - 1], at(y_=off(y, d)))

    def meta_z(d, lane_, i):
        device = at(place_=off(place, d)) if d else at(quad_=next_quad)
        return send(meta.at[lane_], meta.at[lane_], meta_send.at[i], meta_recv.at[i], device)

    for d in range(1, 4):
        near_copy(d).start()
    for d in range(4):
        far_copy(d).start()
    for d in range(1, 4):
        meta_y(d, y).start()

    def unit(i):
        order = [(0, 0), (1, 0), (0, 1), (0, 2), (0, 3), (2, 0), (1, 1), (1, 2), (1, 3), (3, 0), (2, 1), (2, 2), (2, 3), (3, 1), (3, 2), (3, 3)]
        code = jnp.int32(order[0][0] * 4 + order[0][1])
        for n in range(1, ROUNDS):
            code = jnp.where(i == n, order[n][0] * 4 + order[n][1], code)
        kind, step = code // 4, code % 4
        from_quad = jnp.where(kind == 0, quad, jnp.where(kind == 1, 3 - quad, jnp.where(kind == 2, next_quad, 3 - next_quad)))
        return from_quad * 4 + off(place, step), kind, step

    def mate_copy(zz, d):
        ref = kv.at[zz, core, y]
        return send(ref, ref, zs, z_recv.at[zz], at(place_=off(place, d)))

    def quad_copy(zz):
        ref = kv.at[zz, core, y]
        return send(ref, ref, zs, z_recv.at[zz], at(quad_=next_quad))

    def y_copy(zz, d):
        ref = kv.at[zz, core, y]
        return send(ref, ref, ys, y_recv.at[zz], at(y_=off(y, d)))

    def core_copy(zz):
        ref = kv.at[zz, core]
        return send(ref, ref, ss, core_recv.at[zz], at(core_=1 - core))

    def await_bytes(ref, semaphore):
        pltpu.make_async_copy(ref, ref, semaphore).wait()

    def take_in(i):
        zz, kind, step = unit(i)

        @pl.when(i == 0)
        def _():
            for d in range(1, 4):
                near_copy(d, off(x, 4 - d)).wait_recv()

        @pl.when(i == 1)
        def _():
            for d in range(4):
                far_copy(d, True).wait_recv()

        @pl.when(i >= 2)
        def _():
            await_bytes(kv.at[zz, core, y], z_recv.at[zz])

        @pl.when(jnp.logical_and(step == 0, kind < 2))
        def _():
            quad_copy(zz).start()

        @pl.when(step == 0)
        def _():
            for d in range(1, 4):
                mate_copy(zz, d).start()

        for d in (2, 1, 3):
            y_copy(zz, d).start()

    def along_y(i):
        zz, _, _ = unit(i)
        await_bytes(kv.at[zz, core, 0:3], y_recv.at[zz])
        core_copy(zz).start()

    number = lax.broadcasted_iota(jnp.int32, (1, 128), 1)
    token = lax.broadcasted_iota(jnp.int32, (128, 1), 0).astype(jnp.float32)
    query_position = own_block * 128.0 + token

    def key_positions(zz):
        lane_, half_ = zz % 8, zz // 8
        rows = meta[lane_]
        parts = []
        for part in range(4):
            core_, pair = part // 2, part % 2
            low = number < 64
            r = 4 * pair
            hits = jnp.where(low, rows[r:r + 1], rows[r + 2:r + 3])
            block = jnp.where(low, rows[r + 1:r + 2], rows[r + 3:r + 4])
            inner = number % 64
            slot = ((inner // 16) * 32 + half_ * 16 + core_ * 8 + inner % 8).astype(jnp.float32)
            cached = (inner // 8) % 2 == 1
            parts.append(jnp.where(cached, jnp.where(slot < hits, -1.0, DEAD), block * 128.0 + slot))
        return jnp.concatenate(parts, axis=1)

    def absorb(n):
        zz, _, _ = unit(n)
        await_bytes(kv.at[zz, 1 - core], core_recv.at[zz])
        block = kv[zz].reshape(512, 256)
        keys, values = block[:, :HD], block[:, HD:]
        allowed = key_positions(zz) <= query_position
        allowed = jnp.concatenate([allowed] * (TILE // 128), axis=0)

        def tile(t, carry):
            rows = pl.ds(pl.multiple_of(t * TILE, TILE), TILE)
            scores = lax.dot_general(qs[rows], keys, (((1,), (1,)), ((), ())), preferred_element_type=jnp.float32)
            scores = jnp.where(allowed, scores, FLOOR)
            pieces = [scores[:, i * 128:(i + 1) * 128] for i in range(4)]
            old = top[rows]
            new = jnp.maximum(old, jnp.max(functools.reduce(jnp.maximum, pieces), axis=1, keepdims=True))
            top[rows] = new
            factor = jnp.exp2((old - new) * SCALE)
            shift = new * SCALE
            weights = [jnp.exp2(piece * SCALE - shift) for piece in pieces]
            tot[rows] = tot[rows] * factor + functools.reduce(jnp.add, weights)
            rounded = jnp.concatenate([w.astype(jnp.bfloat16) for w in weights], axis=1)
            acc[rows] = acc[rows] * factor + jnp.dot(rounded, values, preferred_element_type=jnp.float32)
            return carry

        lax.fori_loop(0, 1024 // TILE, tile, 0)

    def pick(n, table):
        value = jnp.int32(table[0])
        for i in range(1, len(table)):
            if table[i] != table[i - 1]:
                value = jnp.where(n >= i, table[i], value)
        return value

    def take_in_from(first, last):
        lax.fori_loop(first, last, lambda i, carry: (take_in(i), carry)[1], 0)

    def along_y_from(first, last):
        lax.fori_loop(first, last, lambda i, carry: (along_y(i), carry)[1], 0)

    taken = [6, 10, 11, 12, 13, 14, 15, 16, 16, 16, 16, 16, 16, 16, 16, 16, 16]
    moved = [1, 3, 4, 5, 6, 7, 8, 9, 10, 11, 12, 13, 14, 15, 16, 16, 16]
    next_lane = (next_quad % 2) * 4 + place
    take_in_from(0, taken[0])
    for d in range(1, 4):
        meta_y(d, off(y, 4 - d)).wait_recv()
    for d in range(4):
        meta_z(d, lane, 3 + d).start()
    along_y_from(0, moved[0])
    meta_z(0, next_lane, 3).wait_recv()
    for d in range(1, 4):
        meta_z(d, next_lane, 6 + d).start()

    def rounds(n, carry):
        take_in_from(pick(n, taken), pick(n + 1, taken))
        along_y_from(pick(n, moved), pick(n + 1, moved))

        @pl.when(n == 2)
        def _():
            for d in range(1, 4):
                meta_z(d, (quad % 2) * 4 + off(place, 4 - d), 3 + d).wait_recv()
                meta_z(d, (next_quad % 2) * 4 + off(place, 4 - d), 6 + d).wait_recv()

        absorb(n)
        return carry

    lax.fori_loop(0, ROUNDS, rounds, 0)

    for h in range(8):
        rows = slice(h * 128, (h + 1) * 128)
        total = jnp.sum(tot[rows], axis=1, keepdims=True)
        o_ref[:, rows] = (acc[rows] / total).astype(jnp.bfloat16)

    for d in range(1, 4):
        near_copy(d).wait_send()
        meta_y(d, y).wait_send()
        meta_z(d, next_lane, 6 + d).wait_send()
    for d in range(4):
        far_copy(d).wait_send()
        meta_z(d, lane, 3 + d).wait_send()
    await_bytes(kv.at[0:7, 0, 0:2], zs)
    await_bytes(kv.at[0:12, 0], ys)
    await_bytes(kv.at[:, 0], ss)


def local(queries, new_kv, cache_kv, hit_tokens, block_order):
    dma = pltpu.SemaphoreType.DMA
    return pl.pallas_call(
        kernel,
        out_shape=jax.ShapeDtypeStruct(queries.shape, jnp.bfloat16),
        in_specs=[pl.BlockSpec(memory_space=pltpu.HBM)] * 5,
        out_specs=pl.BlockSpec(memory_space=pltpu.VMEM),
        scratch_shapes=[
            pltpu.VMEM((8, 2048), jnp.bfloat16),
            pltpu.VMEM((8, 2048), jnp.bfloat16),
            pltpu.SMEM((1,), jnp.int32),
            pltpu.SMEM((1,), jnp.int32),
            pltpu.VMEM((16, 2048), jnp.bfloat16),
            pltpu.VMEM((16, 2, 4, 4, 16, 256), jnp.bfloat16),
            pltpu.VMEM((8, 8, 128), jnp.float32),
            pltpu.VMEM((1024, 128), jnp.bfloat16),
            pltpu.VMEM((1024, 128), jnp.float32),
            pltpu.VMEM((1024, 128), jnp.float32),
            pltpu.VMEM((1024, 128), jnp.float32),
            dma((12,)), dma((7,)), dma((7,)), dma((10,)), dma((10,)),
            dma, dma, dma, dma((16,)), dma((16,)), dma((16,)),
        ],
        compiler_params=pltpu.CompilerParams(collective_id=0, has_side_effects=True, vmem_limit_bytes=56 * 1024 * 1024),
        cost_estimate=pl.CostEstimate(flops=4 * 1024 * 8192 * 128, bytes_accessed=1 << 20, transcendentals=1024 * 8192),
    )(queries, new_kv, cache_kv, hit_tokens, block_order)


def solution(mesh):
    in_specs = (P("ctx", "tp"), P(("ctx", "tp"), None), P(("ctx", "tp"), None), P("ctx"), P("ctx"))
    return jax.shard_map(local, mesh=mesh, in_specs=in_specs, out_specs=P("ctx", "tp"), check_vma=False)
```

```python
import functools
import math

import jax
import jax.numpy as jnp
from jax import lax
from jax.experimental import pallas as pl
from jax.experimental.pallas import tpu as pltpu
from jax.sharding import PartitionSpec as P

HD = 128
MESH = pl.DeviceIdType.MESH
FLOOR = -1e30
SCALE = math.log2(math.e) / math.sqrt(HD)
ROUNDS = 16
TILE = 1024
DEAD = 1e9


def kernel(q_ref, new_ref, cache_ref, hits_ref, block_ref, o_ref, new_rows, cache_rows, hits, block, raw, kv, meta, qs, acc, top, tot,
           load_sem, a2a_send, a2a_recv, meta_send, meta_recv, zs, ys, ss, z_recv, y_recv, core_recv):
    ctx, tp = lax.axis_index("ctx"), lax.axis_index("tp")
    lane, y = ctx // 4, ctx % 4
    x, half, core = tp // 4, (tp // 2) % 2, tp % 2
    quad, place = half * 2 + lane // 4, lane % 4
    next_quad = half * 2 + 1 - lane // 4

    def at(x_=None, y_=None, quad_=None, place_=None, core_=None):
        x_ = x if x_ is None else x_
        y_ = y if y_ is None else y_
        quad_ = quad if quad_ is None else quad_
        place_ = place if place_ is None else place_
        core_ = core if core_ is None else core_
        return (((quad_ % 2) * 4 + place_) * 4 + y_, x_ * 4 + (quad_ // 2) * 2 + core_)

    def off(value, d):
        return (value + d) % 4

    barrier = pltpu.get_barrier_semaphore()

    def greet(device):
        pl.semaphore_signal(barrier, inc=1, device_id=device, device_id_type=MESH)

    greet(at(quad_=3 - quad))
    for d in range(1, 4):
        greet(at(x_=off(x, d), quad_=3 - quad))
    greet(at(quad_=next_quad))
    for d in range(1, 4):
        greet(at(place_=off(place, d)))
        greet(at(x_=off(x, d)))
        greet(at(y_=off(y, d)))
    greet(at(core_=1 - core))

    loads = [
        pltpu.make_async_copy(new_ref, new_rows, load_sem.at[0]),
        pltpu.make_async_copy(cache_ref, cache_rows, load_sem.at[1]),
        pltpu.make_async_copy(hits_ref, hits, load_sem.at[2]),
        pltpu.make_async_copy(block_ref, block, load_sem.at[3]),
    ] + [pltpu.make_async_copy(q_ref.at[:, h * 128:(h + 1) * 128], qs.at[h * 128:(h + 1) * 128], load_sem.at[4 + h]) for h in range(8)]
    for load in loads:
        load.start()
    acc[...] = jnp.zeros_like(acc)
    tot[...] = jnp.zeros_like(tot)
    top[...] = jnp.full_like(top, FLOOR)
    for load in loads:
        load.wait()

    raw[...] = jnp.concatenate([new_rows[...], cache_rows[...]], axis=0)
    own_block = block[0].astype(jnp.float32)
    is_hits = lax.broadcasted_iota(jnp.int32, (2, 128), 0) == 0
    meta[lane, pl.ds(y * 2, 2)] = jnp.where(is_hits, hits[0].astype(jnp.float32), own_block)
    own_z = quad * 4 + place
    kv[own_z, core, y, x] = raw[:, pl.ds(pl.multiple_of((x * 2 + half) * 256, 256), 256)]

    pl.semaphore_wait(barrier, 15)

    def send(src, dst, s_sem, r_sem, device):
        return pltpu.make_async_remote_copy(src_ref=src, dst_ref=dst, send_sem=s_sem, recv_sem=r_sem,
                                            device_id=device, device_id_type=MESH)

    def piece(x_, half_):
        return raw.at[:, pl.ds(pl.multiple_of((x_ * 2 + half_) * 256, 256), 256)]

    def near_copy(d, x_from=None):
        x_from = x if x_from is None else x_from
        to = off(x, d)
        return send(piece(to, half), kv.at[own_z, core, y, x_from], a2a_send.at[d - 1], a2a_recv.at[d - 1], at(x_=to))

    def far_copy(d, arriving=False):
        to = off(x, d)
        z_from = (3 - quad) * 4 + place if arriving else own_z
        x_from = off(x, 4 - d) if arriving else x
        return send(piece(to, 1 - half), kv.at[z_from, core, y, x_from], a2a_send.at[d + 3], a2a_recv.at[d + 3], at(x_=to, quad_=3 - quad))

    def meta_y(d, row):
        rows = pl.ds(row * 2, 2)
        return send(meta.at[lane, rows], meta.at[lane, rows], meta_send.at[d - 1], meta_recv.at[d - 1], at(y_=off(y, d)))

    def meta_z(d, lane_, i):
        device = at(place_=off(place, d)) if d else at(quad_=next_quad)
        return send(meta.at[lane_], meta.at[lane_], meta_send.at[i], meta_recv.at[i], device)

    for d in range(1, 4):
        near_copy(d).start()
    for d in range(4):
        far_copy(d).start()
    for d in range(1, 4):
        meta_y(d, y).start()

    def unit(i):
        order = [(0, 0), (1, 0), (0, 1), (0, 2), (0, 3), (2, 0), (1, 1), (1, 2), (1, 3), (3, 0), (2, 1), (2, 2), (2, 3), (3, 1), (3, 2), (3, 3)]
        code = jnp.int32(order[0][0] * 4 + order[0][1])
        for n in range(1, ROUNDS):
            code = jnp.where(i == n, order[n][0] * 4 + order[n][1], code)
        kind, step = code // 4, code % 4
        from_quad = jnp.where(kind == 0, quad, jnp.where(kind == 1, 3 - quad, jnp.where(kind == 2, next_quad, 3 - next_quad)))
        return from_quad * 4 + off(place, step), kind, step

    def mate_copy(zz, d):
        ref = kv.at[zz, core, y]
        return send(ref, ref, zs, z_recv.at[zz], at(place_=off(place, d)))

    def quad_copy(zz):
        ref = kv.at[zz, core, y]
        return send(ref, ref, zs, z_recv.at[zz], at(quad_=next_quad))

    def y_copy(zz, d):
        ref = kv.at[zz, core, y]
        return send(ref, ref, ys, y_recv.at[zz], at(y_=off(y, d)))

    def core_copy(zz):
        ref = kv.at[zz, core]
        return send(ref, ref, ss, core_recv.at[zz], at(core_=1 - core))

    def await_bytes(ref, semaphore):
        pltpu.make_async_copy(ref, ref, semaphore).wait()

    def take_in(i):
        zz, kind, step = unit(i)

        @pl.when(i == 0)
        def _():
            for d in range(1, 4):
                near_copy(d, off(x, 4 - d)).wait_recv()

        @pl.when(i == 1)
        def _():
            for d in range(4):
                far_copy(d, True).wait_recv()

        @pl.when(i >= 2)
        def _():
            await_bytes(kv.at[zz, core, y], z_recv.at[zz])

        @pl.when(jnp.logical_and(step == 0, kind < 2))
        def _():
            quad_copy(zz).start()

        @pl.when(step == 0)
        def _():
            for d in range(1, 4):
                mate_copy(zz, d).start()

        for d in (2, 1, 3):
            y_copy(zz, d).start()

    def along_y(i):
        zz, _, _ = unit(i)
        await_bytes(kv.at[zz, core, 0:3], y_recv.at[zz])
        core_copy(zz).start()

    number = lax.broadcasted_iota(jnp.int32, (1, 128), 1)
    token = lax.broadcasted_iota(jnp.int32, (128, 1), 0).astype(jnp.float32)
    query_position = own_block * 128.0 + token

    def key_positions(zz):
        lane_, half_ = zz % 8, zz // 8
        rows = meta[lane_]
        parts = []
        for part in range(4):
            core_, pair = part // 2, part % 2
            low = number < 64
            r = 4 * pair
            hits = jnp.where(low, rows[r:r + 1], rows[r + 2:r + 3])
            block = jnp.where(low, rows[r + 1:r + 2], rows[r + 3:r + 4])
            inner = number % 64
            slot = ((inner // 16) * 32 + half_ * 16 + core_ * 8 + inner % 8).astype(jnp.float32)
            cached = (inner // 8) % 2 == 1
            parts.append(jnp.where(cached, jnp.where(slot < hits, -1.0, DEAD), block * 128.0 + slot))
        return jnp.concatenate(parts, axis=1)

    def absorb(n):
        zz, _, _ = unit(n)
        await_bytes(kv.at[zz, 1 - core], core_recv.at[zz])
        block = kv[zz].reshape(512, 256)
        keys, values = block[:, :HD], block[:, HD:]
        allowed = key_positions(zz) <= query_position
        allowed = jnp.concatenate([allowed] * (TILE // 128), axis=0)

        def tile(t, carry):
            rows = pl.ds(pl.multiple_of(t * TILE, TILE), TILE)
            scores = lax.dot_general(qs[rows], keys, (((1,), (1,)), ((), ())), preferred_element_type=jnp.float32)
            scores = jnp.where(allowed, scores, FLOOR)
            pieces = [scores[:, i * 128:(i + 1) * 128] for i in range(4)]
            old = top[rows]
            new = jnp.maximum(old, jnp.max(functools.reduce(jnp.maximum, pieces), axis=1, keepdims=True))
            top[rows] = new
            factor = jnp.exp2((old - new) * SCALE)
            shift = new * SCALE
            weights = [jnp.exp2(piece * SCALE - shift) for piece in pieces]
            tot[rows] = tot[rows] * factor + functools.reduce(jnp.add, weights)
            rounded = jnp.concatenate([w.astype(jnp.bfloat16) for w in weights], axis=1)
            acc[rows] = acc[rows] * factor + jnp.dot(rounded, values, preferred_element_type=jnp.float32)
            return carry

        lax.fori_loop(0, 1024 // TILE, tile, 0)

    def pick(n, table):
        value = jnp.int32(table[0])
        for i in range(1, len(table)):
            if table[i] != table[i - 1]:
                value = jnp.where(n >= i, table[i], value)
        return value

    def take_in_from(first, last):
        lax.fori_loop(first, last, lambda i, carry: (take_in(i), carry)[1], 0)

    def along_y_from(first, last):
        lax.fori_loop(first, last, lambda i, carry: (along_y(i), carry)[1], 0)

    taken = [6, 10, 11, 12, 13, 14, 15, 16, 16, 16, 16, 16, 16, 16, 16, 16, 16]
    moved = [1, 3, 4, 5, 6, 7, 8, 9, 10, 11, 12, 13, 14, 15, 16, 16, 16]
    next_lane = (next_quad % 2) * 4 + place
    take_in_from(0, 1)
    for d in range(1, 4):
        meta_y(d, off(y, 4 - d)).wait_recv()
    for d in range(4):
        meta_z(d, lane, 3 + d).start()
    take_in_from(1, taken[0])
    along_y_from(0, moved[0])
    meta_z(0, next_lane, 3).wait_recv()
    for d in range(1, 4):
        meta_z(d, next_lane, 6 + d).start()

    def rounds(n, carry):
        take_in_from(pick(n, taken), pick(n + 1, taken))
        along_y_from(pick(n, moved), pick(n + 1, moved))

        @pl.when(n == 2)
        def _():
            for d in range(1, 4):
                meta_z(d, (quad % 2) * 4 + off(place, 4 - d), 3 + d).wait_recv()
                meta_z(d, (next_quad % 2) * 4 + off(place, 4 - d), 6 + d).wait_recv()

        absorb(n)
        return carry

    lax.fori_loop(0, ROUNDS, rounds, 0)

    for h in range(8):
        rows = slice(h * 128, (h + 1) * 128)
        total = jnp.sum(tot[rows], axis=1, keepdims=True)
        o_ref[:, rows] = (acc[rows] / total).astype(jnp.bfloat16)

    for d in range(1, 4):
        near_copy(d).wait_send()
        meta_y(d, y).wait_send()
        meta_z(d, next_lane, 6 + d).wait_send()
    for d in range(4):
        far_copy(d).wait_send()
        meta_z(d, lane, 3 + d).wait_send()
    await_bytes(kv.at[0:7, 0, 0:2], zs)
    await_bytes(kv.at[0:12, 0], ys)
    await_bytes(kv.at[:, 0], ss)


def local(queries, new_kv, cache_kv, hit_tokens, block_order):
    dma = pltpu.SemaphoreType.DMA
    return pl.pallas_call(
        kernel,
        out_shape=jax.ShapeDtypeStruct(queries.shape, jnp.bfloat16),
        in_specs=[pl.BlockSpec(memory_space=pltpu.HBM)] * 5,
        out_specs=pl.BlockSpec(memory_space=pltpu.VMEM),
        scratch_shapes=[
            pltpu.VMEM((8, 2048), jnp.bfloat16),
            pltpu.VMEM((8, 2048), jnp.bfloat16),
            pltpu.SMEM((1,), jnp.int32),
            pltpu.SMEM((1,), jnp.int32),
            pltpu.VMEM((16, 2048), jnp.bfloat16),
            pltpu.VMEM((16, 2, 4, 4, 16, 256), jnp.bfloat16),
            pltpu.VMEM((8, 8, 128), jnp.float32),
            pltpu.VMEM((1024, 128), jnp.bfloat16),
            pltpu.VMEM((1024, 128), jnp.float32),
            pltpu.VMEM((1024, 128), jnp.float32),
            pltpu.VMEM((1024, 128), jnp.float32),
            dma((12,)), dma((7,)), dma((7,)), dma((10,)), dma((10,)),
            dma, dma, dma, dma((16,)), dma((16,)), dma((16,)),
        ],
        compiler_params=pltpu.CompilerParams(collective_id=0, has_side_effects=True, vmem_limit_bytes=56 * 1024 * 1024),
        cost_estimate=pl.CostEstimate(flops=4 * 1024 * 8192 * 128, bytes_accessed=1 << 20, transcendentals=1024 * 8192),
    )(queries, new_kv, cache_kv, hit_tokens, block_order)


def solution(mesh):
    in_specs = (P("ctx", "tp"), P(("ctx", "tp"), None), P(("ctx", "tp"), None), P("ctx"), P("ctx"))
    return jax.shard_map(local, mesh=mesh, in_specs=in_specs, out_specs=P("ctx", "tp"), check_vma=False)
```

```python
import functools
import math

import jax
import jax.numpy as jnp
from jax import lax
from jax.experimental import pallas as pl
from jax.experimental.pallas import tpu as pltpu
from jax.sharding import PartitionSpec as P

HD = 128
MESH = pl.DeviceIdType.MESH
FLOOR = -1e30
SCALE = math.log2(math.e) / math.sqrt(HD)
ROUNDS = 16
TILE = 1024
DEAD = 1e9


def kernel(q_ref, new_ref, cache_ref, hits_ref, block_ref, o_ref, new_rows, cache_rows, hits, block, raw, kv, meta, qs, acc, top, tot,
           load_sem, a2a_send, a2a_recv, meta_send, meta_recv, zs, ys, ss, z_recv, y_recv, core_recv):
    ctx, tp = lax.axis_index("ctx"), lax.axis_index("tp")
    lane, y = ctx // 4, ctx % 4
    x, half, core = tp // 4, (tp // 2) % 2, tp % 2
    quad, place = half * 2 + lane // 4, lane % 4
    next_quad = half * 2 + 1 - lane // 4

    def at(x_=None, y_=None, quad_=None, place_=None, core_=None):
        x_ = x if x_ is None else x_
        y_ = y if y_ is None else y_
        quad_ = quad if quad_ is None else quad_
        place_ = place if place_ is None else place_
        core_ = core if core_ is None else core_
        return (((quad_ % 2) * 4 + place_) * 4 + y_, x_ * 4 + (quad_ // 2) * 2 + core_)

    def off(value, d):
        return (value + d) % 4

    barrier = pltpu.get_barrier_semaphore()

    def greet(device):
        pl.semaphore_signal(barrier, inc=1, device_id=device, device_id_type=MESH)

    greet(at(quad_=3 - quad))
    for d in range(1, 4):
        greet(at(x_=off(x, d), quad_=3 - quad))
    greet(at(quad_=next_quad))
    for d in range(1, 4):
        greet(at(place_=off(place, d)))
        greet(at(x_=off(x, d)))
        greet(at(y_=off(y, d)))
    greet(at(core_=1 - core))

    loads = [
        pltpu.make_async_copy(new_ref, new_rows, load_sem.at[0]),
        pltpu.make_async_copy(cache_ref, cache_rows, load_sem.at[1]),
        pltpu.make_async_copy(hits_ref, hits, load_sem.at[2]),
        pltpu.make_async_copy(block_ref, block, load_sem.at[3]),
    ] + [pltpu.make_async_copy(q_ref.at[:, h * 128:(h + 1) * 128], qs.at[h * 128:(h + 1) * 128], load_sem.at[4 + h]) for h in range(8)]
    for load in loads:
        load.start()
    acc[...] = jnp.zeros_like(acc)
    tot[...] = jnp.zeros_like(tot)
    top[...] = jnp.full_like(top, FLOOR)
    for load in loads:
        load.wait()

    raw[...] = jnp.concatenate([new_rows[...], cache_rows[...]], axis=0)
    own_block = block[0].astype(jnp.float32)
    is_hits = lax.broadcasted_iota(jnp.int32, (2, 128), 0) == 0
    meta[lane, pl.ds(y * 2, 2)] = jnp.where(is_hits, hits[0].astype(jnp.float32), own_block)
    own_z = quad * 4 + place
    kv[own_z, core, y, x] = raw[:, pl.ds(pl.multiple_of((x * 2 + half) * 256, 256), 256)]

    pl.semaphore_wait(barrier, 15)

    def send(src, dst, s_sem, r_sem, device):
        return pltpu.make_async_remote_copy(src_ref=src, dst_ref=dst, send_sem=s_sem, recv_sem=r_sem,
                                            device_id=device, device_id_type=MESH)

    def piece(x_, half_):
        return raw.at[:, pl.ds(pl.multiple_of((x_ * 2 + half_) * 256, 256), 256)]

    def near_copy(d, x_from=None):
        x_from = x if x_from is None else x_from
        to = off(x, d)
        return send(piece(to, half), kv.at[own_z, core, y, x_from], a2a_send.at[d - 1], a2a_recv.at[d - 1], at(x_=to))

    def far_copy(d, arriving=False):
        to = off(x, d)
        z_from = (3 - quad) * 4 + place if arriving else own_z
        x_from = off(x, 4 - d) if arriving else x
        return send(piece(to, 1 - half), kv.at[z_from, core, y, x_from], a2a_send.at[d + 3], a2a_recv.at[d + 3], at(x_=to, quad_=3 - quad))

    def meta_y(d, row):
        rows = pl.ds(row * 2, 2)
        return send(meta.at[lane, rows], meta.at[lane, rows], meta_send.at[d - 1], meta_recv.at[d - 1], at(y_=off(y, d)))

    def meta_z(d, lane_, i):
        device = at(place_=off(place, d)) if d else at(quad_=next_quad)
        return send(meta.at[lane_], meta.at[lane_], meta_send.at[i], meta_recv.at[i], device)

    for d in range(1, 4):
        near_copy(d).start()
    for d in range(4):
        far_copy(d).start()
    for d in range(1, 4):
        meta_y(d, y).start()

    def unit(i):
        order = [(0, 0), (1, 0), (0, 1), (0, 2), (0, 3), (2, 0), (1, 1), (1, 2), (1, 3), (3, 0), (2, 1), (2, 2), (2, 3), (3, 1), (3, 2), (3, 3)]
        code = jnp.int32(order[0][0] * 4 + order[0][1])
        for n in range(1, ROUNDS):
            code = jnp.where(i == n, order[n][0] * 4 + order[n][1], code)
        kind, step = code // 4, code % 4
        from_quad = jnp.where(kind == 0, quad, jnp.where(kind == 1, 3 - quad, jnp.where(kind == 2, next_quad, 3 - next_quad)))
        return from_quad * 4 + off(place, step), kind, step

    def mate_copy(zz, d):
        ref = kv.at[zz, core, y]
        return send(ref, ref, zs, z_recv.at[zz], at(place_=off(place, d)))

    def quad_copy(zz):
        ref = kv.at[zz, core, y]
        return send(ref, ref, zs, z_recv.at[zz], at(quad_=next_quad))

    def y_copy(zz, d):
        ref = kv.at[zz, core, y]
        return send(ref, ref, ys, y_recv.at[zz], at(y_=off(y, d)))

    def core_copy(zz):
        ref = kv.at[zz, core]
        return send(ref, ref, ss, core_recv.at[zz], at(core_=1 - core))

    def await_bytes(ref, semaphore):
        pltpu.make_async_copy(ref, ref, semaphore).wait()

    def take_in(i):
        zz, kind, step = unit(i)

        @pl.when(i == 0)
        def _():
            for d in range(1, 4):
                near_copy(d, off(x, 4 - d)).wait_recv()

        @pl.when(i == 1)
        def _():
            for d in range(4):
                far_copy(d, True).wait_recv()

        @pl.when(i >= 2)
        def _():
            await_bytes(kv.at[zz, core, y], z_recv.at[zz])

        @pl.when(jnp.logical_and(step == 0, kind < 2))
        def _():
            quad_copy(zz).start()

        @pl.when(step == 0)
        def _():
            for d in range(1, 4):
                mate_copy(zz, d).start()

        for d in (2, 1, 3):
            y_copy(zz, d).start()

    def along_y(i):
        zz, _, _ = unit(i)
        await_bytes(kv.at[zz, core, 0:3], y_recv.at[zz])
        core_copy(zz).start()

    number = lax.broadcasted_iota(jnp.int32, (1, 128), 1)
    token = lax.broadcasted_iota(jnp.int32, (128, 1), 0).astype(jnp.float32)
    query_position = own_block * 128.0 + token

    def key_positions(zz):
        lane_, half_ = zz % 8, zz // 8
        rows = meta[lane_]
        parts = []
        for part in range(4):
            core_, pair = part // 2, part % 2
            low = number < 64
            r = 4 * pair
            hits = jnp.where(low, rows[r:r + 1], rows[r + 2:r + 3])
            block = jnp.where(low, rows[r + 1:r + 2], rows[r + 3:r + 4])
            inner = number % 64
            slot = ((inner // 16) * 32 + half_ * 16 + core_ * 8 + inner % 8).astype(jnp.float32)
            cached = (inner // 8) % 2 == 1
            parts.append(jnp.where(cached, jnp.where(slot < hits, -1.0, DEAD), block * 128.0 + slot))
        return jnp.concatenate(parts, axis=1)

    def absorb(n):
        zz, _, _ = unit(n)
        await_bytes(kv.at[zz, 1 - core], core_recv.at[zz])
        block = kv[zz].reshape(512, 256)
        keys, values = block[:, :HD], block[:, HD:]
        allowed = key_positions(zz) <= query_position
        allowed = jnp.concatenate([allowed] * (TILE // 128), axis=0)

        def tile(t, carry):
            rows = pl.ds(pl.multiple_of(t * TILE, TILE), TILE)
            scores = lax.dot_general(qs[rows], keys, (((1,), (1,)), ((), ())), preferred_element_type=jnp.float32)
            scores = jnp.where(allowed, scores, FLOOR)
            pieces = [scores[:, i * 128:(i + 1) * 128] for i in range(4)]
            old = top[rows]
            new = jnp.maximum(old, jnp.max(functools.reduce(jnp.maximum, pieces), axis=1, keepdims=True))
            top[rows] = new
            factor = jnp.exp2((old - new) * SCALE)
            shift = new * SCALE
            weights = [jnp.exp2(piece * SCALE - shift) for piece in pieces]
            tot[rows] = tot[rows] * factor + functools.reduce(jnp.add, weights)
            rounded = jnp.concatenate([w.astype(jnp.bfloat16) for w in weights], axis=1)
            acc[rows] = acc[rows] * factor + jnp.dot(rounded, values, preferred_element_type=jnp.float32)
            return carry

        lax.fori_loop(0, 1024 // TILE, tile, 0)

    def pick(n, table):
        value = jnp.int32(table[0])
        for i in range(1, len(table)):
            if table[i] != table[i - 1]:
                value = jnp.where(n >= i, table[i], value)
        return value

    def take_in_from(first, last):
        lax.fori_loop(first, last, lambda i, carry: (take_in(i), carry)[1], 0)

    def along_y_from(first, last):
        lax.fori_loop(first, last, lambda i, carry: (along_y(i), carry)[1], 0)

    taken = [6, 10, 11, 12, 13, 14, 15, 16, 16, 16, 16, 16, 16, 16, 16, 16, 16]
    moved = [1, 3, 4, 5, 6, 7, 8, 9, 10, 11, 12, 13, 14, 15, 16, 16, 16]
    next_lane = (next_quad % 2) * 4 + place
    take_in_from(0, 1)
    for d in range(1, 4):
        meta_y(d, off(y, 4 - d)).wait_recv()
    for d in range(4):
        meta_z(d, lane, 3 + d).start()
    take_in_from(1, taken[0])
    meta_z(0, next_lane, 3).wait_recv()
    for d in range(1, 4):
        meta_z(d, next_lane, 6 + d).start()
    along_y_from(0, moved[0])

    def rounds(n, carry):
        take_in_from(pick(n, taken), pick(n + 1, taken))
        along_y_from(pick(n, moved), pick(n + 1, moved))

        @pl.when(n == 2)
        def _():
            for d in range(1, 4):
                meta_z(d, (quad % 2) * 4 + off(place, 4 - d), 3 + d).wait_recv()
                meta_z(d, (next_quad % 2) * 4 + off(place, 4 - d), 6 + d).wait_recv()

        absorb(n)
        return carry

    lax.fori_loop(0, ROUNDS, rounds, 0)

    for h in range(8):
        rows = slice(h * 128, (h + 1) * 128)
        total = jnp.sum(tot[rows], axis=1, keepdims=True)
        o_ref[:, rows] = (acc[rows] / total).astype(jnp.bfloat16)

    for d in range(1, 4):
        near_copy(d).wait_send()
        meta_y(d, y).wait_send()
        meta_z(d, next_lane, 6 + d).wait_send()
    for d in range(4):
        far_copy(d).wait_send()
        meta_z(d, lane, 3 + d).wait_send()
    await_bytes(kv.at[0:7, 0, 0:2], zs)
    await_bytes(kv.at[0:12, 0], ys)
    await_bytes(kv.at[:, 0], ss)


def local(queries, new_kv, cache_kv, hit_tokens, block_order):
    dma = pltpu.SemaphoreType.DMA
    return pl.pallas_call(
        kernel,
        out_shape=jax.ShapeDtypeStruct(queries.shape, jnp.bfloat16),
        in_specs=[pl.BlockSpec(memory_space=pltpu.HBM)] * 5,
        out_specs=pl.BlockSpec(memory_space=pltpu.VMEM),
        scratch_shapes=[
            pltpu.VMEM((8, 2048), jnp.bfloat16),
            pltpu.VMEM((8, 2048), jnp.bfloat16),
            pltpu.SMEM((1,), jnp.int32),
            pltpu.SMEM((1,), jnp.int32),
            pltpu.VMEM((16, 2048), jnp.bfloat16),
            pltpu.VMEM((16, 2, 4, 4, 16, 256), jnp.bfloat16),
            pltpu.VMEM((8, 8, 128), jnp.float32),
            pltpu.VMEM((1024, 128), jnp.bfloat16),
            pltpu.VMEM((1024, 128), jnp.float32),
            pltpu.VMEM((1024, 128), jnp.float32),
            pltpu.VMEM((1024, 128), jnp.float32),
            dma((12,)), dma((7,)), dma((7,)), dma((10,)), dma((10,)),
            dma, dma, dma, dma((16,)), dma((16,)), dma((16,)),
        ],
        compiler_params=pltpu.CompilerParams(collective_id=0, has_side_effects=True, vmem_limit_bytes=56 * 1024 * 1024),
        cost_estimate=pl.CostEstimate(flops=4 * 1024 * 8192 * 128, bytes_accessed=1 << 20, transcendentals=1024 * 8192),
    )(queries, new_kv, cache_kv, hit_tokens, block_order)


def solution(mesh):
    in_specs = (P("ctx", "tp"), P(("ctx", "tp"), None), P(("ctx", "tp"), None), P("ctx"), P("ctx"))
    return jax.shard_map(local, mesh=mesh, in_specs=in_specs, out_specs=P("ctx", "tp"), check_vma=False)
```
